256 devices in a mesh: rows: 64 (over x_lo, y, z), heads: 4 (over x_hi, core).
Axes of the slice: x: 4 (x_hi: 2, x_lo: 2; x = x_hi * 2 + x_lo), y: 4, z: 8, core: 2. Of those that a mesh axis runs over, the one named last changes fastest.
Arguments:
- new_qkv: bfloat16 [3, 49152, 5120], P(None, 'rows', 'heads'), may hold values from -1000 to 1000
- cache_kv: bfloat16 [2, 65536, 5120], P(None, 'rows', 'heads'), may hold values from -6 to 6
- q_gain: float32 [5120], P('heads'), may hold values from 0.5 to 1.5
- k_gain: float32 [5120], P('heads'), may hold values from 0.5 to 1.5
- new_list: int32 [384, 3], P('rows'), may hold values from 0 to 383, as said below
- new_count: int32 [384], P('rows'), may hold values from 1 to 3
- cache_list: int32 [384, 5], P('rows'), may hold values from 0 to 511, as said below
- cache_count: int32 [384], P('rows'), may hold values from 1 to 5
Outputs:
- attended: bfloat16 [49152, 5120], P('rows', 'heads')
The draws below stay inside these ranges and needn't reach their ends.
Inputs may be any that keep to these rules, and one draw needn't show every extreme that they name: `new_list`: entry 0 of row t is t itself; the next new_count[t] - 1 entries are distinct tiles among t - 1 and t + 1; later entries repeat t. The first and the last query tile of each row shard list both adjacent tiles where they exist. `cache_list`: the live entries of row t are distinct cache tiles of the query tile's own row shard, or lie within 2 tiles beyond that shard's lower or upper edge; later entries repeat entry 0. The first and the last query tile of each row shard list min(5, available) tiles, the first one reaching below its shard where that exists, the last one above.
All inputs are finite; a program needn't handle non-finite values.
Results may differ from the reference program's by a relative error of at most 0.0085.
Values may be sent and summed in bfloat16 or wider, within the bound.
A program may use at most 128 MiB of HBM per device.

```python
import math
import jax
import jax.numpy as jnp
from jax import lax

HEADS = 40
HEAD_DIM = 128
WIDTH = 5120
TILE = 128
MAXC = 3
MAXK = 5
CREACH = 2
QT_DEV = 6
KT_DEV = 8
QTILES = 384
CTILES = 512
NC = 65536


def fresh_tables(key):
    key = jax.random.fold_in(key, 101)
    key_keep, key_swap = jax.random.split(key, 2)
    tile_ids = jnp.arange(QTILES, dtype=jnp.int32)
    position = tile_ids % QT_DEV
    at_edge = (position == 0) | (position == QT_DEV - 1)
    keep = jax.random.randint(key_keep, (QTILES, 2), 0, 4) > 0
    keep = keep | at_edge[:, None]
    neighbours = jnp.stack([tile_ids - 1, tile_ids + 1], axis=1)
    exists = (neighbours >= 0) & (neighbours < QTILES)
    usable = keep & exists
    swapped = jax.random.randint(key_swap, (QTILES,), 0, 2) == 1
    first_pick = jnp.where(swapped, neighbours[:, 1], neighbours[:, 0])
    second_pick = jnp.where(swapped, neighbours[:, 0], neighbours[:, 1])
    first_live = jnp.where(swapped, usable[:, 1], usable[:, 0])
    second_live = jnp.where(swapped, usable[:, 0], usable[:, 1])
    entry_one = jnp.where(first_live, first_pick, jnp.where(second_live, second_pick, tile_ids))
    entry_two = jnp.where(first_live & second_live, second_pick, tile_ids)
    tables = jnp.stack([tile_ids, entry_one, entry_two], axis=1).astype(jnp.int32)
    counts = (1 + first_live.astype(jnp.int32) + second_live.astype(jnp.int32)).astype(jnp.int32)
    return (tables, counts)


def cache_tables(key):
    key = jax.random.fold_in(key, 202)
    key_coin, key_prio, key_count = jax.random.split(key, 3)
    tile_ids = jnp.arange(QTILES, dtype=jnp.int32)
    device_of = tile_ids // QT_DEV
    position = tile_ids % QT_DEV
    is_first = position == 0
    is_last = position == QT_DEV - 1
    coin = jax.random.randint(key_coin, (QTILES,), 0, 2)
    use_low = is_first | ~is_last & (coin == 0)
    use_high = is_last | ~is_first & (coin == 1)
    candidates = KT_DEV + 2 * CREACH
    slots = jnp.arange(candidates, dtype=jnp.int32)
    target = device_of[:, None] * KT_DEV - CREACH + slots[None, :]
    in_low = slots[None, :] < CREACH
    in_high = slots[None, :] >= CREACH + KT_DEV
    usable = (target >= 0) & (target < CTILES) & (~in_low | use_low[:, None]) & (~in_high | use_high[:, None])
    priority = jax.random.randint(key_prio, (QTILES, candidates), 0, 1 << 20) * candidates + slots[None, :]
    priority = priority + jnp.where(usable, 0, 1 << 28)
    order = jnp.argsort(priority, axis=1, stable=True)
    picked = jnp.take_along_axis(target, order, axis=1)[:, :MAXK]
    available = jnp.sum(usable.astype(jnp.int32), axis=1)
    counts = jax.random.randint(key_count, (QTILES,), 1, MAXK + 1)
    counts = jnp.where(is_first | is_last, MAXK, counts)
    counts = jnp.minimum(counts, available).astype(jnp.int32)
    live = jnp.arange(MAXK, dtype=jnp.int32)[None, :] < counts[:, None]
    tables = jnp.where(live, picked, picked[:, :1]).astype(jnp.int32)
    return (tables, counts)


def draw_new_list(key, part):
    shared = fresh_tables(key)
    return shared[0]


def draw_new_count(key, part):
    shared = fresh_tables(key)
    return shared[1]


def draw_cache_list(key, part):
    shared = cache_tables(key)
    return shared[0]


def draw_cache_count(key, part):
    shared = cache_tables(key)
    return shared[1]


def draw_new_qkv(key, part):
    key = jax.random.fold_in(key, 5)
    key_base, key_rough, key_rows = jax.random.split(key, 3)
    total_rows = QTILES * TILE
    columns = HEADS * HEAD_DIM
    column_place = jnp.arange(columns, dtype=jnp.float32) / columns
    rate = 1.5
    base = jax.random.truncated_normal(key_base, -4.0, 4.0, (3, total_rows, columns), jnp.float32)
    rough = jnp.exp(jax.random.uniform(key_rough, (2, 1, columns), jnp.float32, 0.0, math.log(10.0)))
    rising = jnp.exp(0.5 * rate * column_place)[None, None, :]
    row_scale = jnp.exp(jax.random.uniform(key_rows, (2, total_rows, 1), jnp.float32, 0.0, math.log(10.0)))
    features = base[:2] * rough * rising * row_scale
    return jnp.concatenate([features, base[2:]], axis=0).astype(jnp.bfloat16)


def shard_levels(stream_key, dims, pieces, least, high):
    loudness = 1.0
    for dim, blocks in pieces:
        heights = jax.random.uniform(jax.random.fold_in(jax.random.fold_in(stream_key, 6), dim), (blocks,), jnp.float32, least / len(pieces), high / len(pieces))
        loudness = loudness * jnp.repeat(jnp.exp(heights), dims[dim] // blocks).reshape((-1,) + (1,) * (len(dims) - 1 - dim))
    return loudness


def centred(key, extent, scale, most, pieces=(), kind=jnp.bfloat16):
    factor_of = shard_levels(key, extent, pieces, -0.22, 0.18) if pieces else 1.0
    values = jax.random.normal(key, extent, jnp.float32) * scale * factor_of
    return jnp.minimum(jnp.maximum(values, -most), most).astype(kind)


def setup_inputs(seed: int = 0) -> dict:
    arg_keys = jax.random.split(jax.random.key(seed), 9)
    return {
        "new_qkv": draw_new_qkv(jax.random.fold_in(arg_keys[8], 71), 0),
        "cache_kv": centred(arg_keys[1], (2, NC, WIDTH), 1.0, 6.0, ((1, 64), (2, 4))),
        "q_gain": jnp.clip(1.0 + 0.1 * jax.random.normal(arg_keys[2], (WIDTH,), jnp.float32), 0.5, 1.5),
        "k_gain": jnp.clip(1.0 + 0.1 * jax.random.normal(arg_keys[3], (WIDTH,), jnp.float32), 0.5, 1.5),
        "new_list": draw_new_list(jax.random.fold_in(arg_keys[8], 71), 0),
        "new_count": draw_new_count(jax.random.fold_in(arg_keys[8], 71), 0),
        "cache_list": draw_cache_list(jax.random.fold_in(arg_keys[8], 71), 0),
        "cache_count": draw_cache_count(jax.random.fold_in(arg_keys[8], 71), 0),
    }


def norm_rows(values, gains):
    wide = values.astype(jnp.float32)
    square_mean = lax.optimization_barrier(jnp.mean(wide * wide, axis=-1, keepdims=True))
    return (wide * lax.rsqrt(square_mean + 1e-06) * gains).astype(jnp.bfloat16)

def reference(new_qkv, cache_kv, q_gain, k_gain, new_list, new_count, cache_list, cache_count):
    q_tiles = new_qkv[0].reshape(QTILES, TILE, WIDTH)
    k_tiles = new_qkv[1].reshape(QTILES, TILE, WIDTH)
    v_tiles = new_qkv[2].reshape(QTILES, TILE, WIDTH)
    ck_tiles = cache_kv[0].reshape(CTILES, TILE, WIDTH)
    cv_tiles = cache_kv[1].reshape(CTILES, TILE, WIDTH)
    score_scale = HEAD_DIM ** (-0.5)

    def one_tile(tile_id):
        queries = norm_rows(q_tiles[tile_id], q_gain).astype(jnp.float32).reshape(TILE, HEADS, HEAD_DIM)
        near_ids = new_list[tile_id]
        far_ids = cache_list[tile_id]
        near_keys = norm_rows(k_tiles[near_ids].reshape(MAXC * TILE, WIDTH), k_gain)
        far_keys = ck_tiles[far_ids].reshape(MAXK * TILE, WIDTH)
        all_keys = jnp.concatenate([near_keys, far_keys], axis=0).astype(jnp.float32).reshape(-1, HEADS, HEAD_DIM)
        near_vals = v_tiles[near_ids].reshape(MAXC * TILE, WIDTH)
        far_vals = cv_tiles[far_ids].reshape(MAXK * TILE, WIDTH)
        all_vals = jnp.concatenate([near_vals, far_vals], axis=0).astype(jnp.float32).reshape(-1, HEADS, HEAD_DIM)
        near_live = jnp.repeat(jnp.arange(MAXC, dtype=jnp.int32) < new_count[tile_id], TILE)
        far_live = jnp.repeat(jnp.arange(MAXK, dtype=jnp.int32) < cache_count[tile_id], TILE)
        live_keys = jnp.concatenate([near_live, far_live])
        scores = jnp.einsum('qhd,khd->hqk', queries, all_keys) * score_scale
        scores = jnp.where(live_keys[None, None, :], scores, -jnp.inf)
        row_max = lax.optimization_barrier(jnp.max(scores, axis=2, keepdims=True))
        weights = jnp.exp(scores - row_max)
        row_total = lax.optimization_barrier(jnp.sum(weights, axis=2, keepdims=True))
        weights_bf = (weights / row_total).astype(jnp.bfloat16)
        mixed = jnp.einsum('hqk,khd->qhd', weights_bf.astype(jnp.float32), all_vals)
        return mixed.reshape(TILE, WIDTH).astype(jnp.bfloat16)
    blocks = lax.map(one_tile, jnp.arange(QTILES, dtype=jnp.int32))
    return blocks.reshape(QTILES * TILE, WIDTH)
```

```python
import functools

import jax
import jax.numpy as jnp
from jax import lax
from jax.experimental import pallas as pl
from jax.experimental.pallas import tpu as pltpu
from jax.sharding import PartitionSpec as P

HEADS = 40
HEAD_DIM = 128
TILE = 128
REACH = 2
CHUNKS = (2, 2, 2, 2, 1, 1)
EARLY = 3
MESH = pl.DeviceIdType.MESH


def kernel(
    new_list, new_count, cache_list, cache_count, q_gain, k_gain, new_qkv, cache_tiles, out, *scratch
):
    n_chunks = len(CHUNKS)
    news, caches = scratch[:n_chunks], scratch[n_chunks : 2 * n_chunks]
    (raw, q_scale, k_scale, halo_scale, sums, peer_sums, rates, halo_rates, bias, mixed) = scratch[
        2 * n_chunks : 2 * n_chunks + 10
    ]
    (raw_sem, local_sem, far_send, far_recv, near_send, near_recv, sum_send, sum_recv,
     rate_send, rate_recv, out_sem) = scratch[2 * n_chunks + 10 :]
    row, group = lax.axis_index("rows"), lax.axis_index("heads")
    n_rows, n_groups = lax.axis_size("rows"), lax.axis_size("heads")
    above, below = lax.rem(row + 1, n_rows), lax.rem(row + n_rows - 1, n_rows)
    peers = [lax.rem(group + step, n_groups) for step in range(1, n_groups)]
    rows_here, width = new_qkv.shape[1:]
    cache_count_here = cache_tiles.shape[1]
    tiles = rows_here // TILE
    heads = width // HEAD_DIM
    place = [(chunk, at) for chunk, count in enumerate(CHUNKS) for at in range(count)]

    def columns(head):
        return pl.ds(head * HEAD_DIM, HEAD_DIM)

    def local(source, target, sem):
        copy = pltpu.make_async_copy(source, target, sem)
        copy.start()
        return copy

    def remote(source, target, send, recv, device):
        return pltpu.make_async_remote_copy(
            src_ref=source, dst_ref=target, send_sem=send, recv_sem=recv,
            device_id=device, device_id_type=MESH,
        )

    raw_copies = [
        local(
            new_qkv.at[pl.ds(0, 2), pl.ds(t * TILE, TILE)],
            raw.at[:, pl.ds(t * TILE, TILE)],
            raw_sem.at[t],
        )
        for t in range(tiles)
    ]

    barrier = pltpu.get_barrier_semaphore()
    for device in [(above, group), (below, group)] + [(row, peer) for peer in peers]:
        pl.semaphore_signal(barrier, inc=1, device_id=device, device_id_type=MESH)
    pl.semaphore_wait(barrier, n_groups + 1)

    far, near = [], []
    for head, (chunk, at) in enumerate(place):
        cols = columns(head)
        there, edge = caches[chunk].at[at], news[chunk].at[at]
        far.append(
            (
                remote(
                    cache_tiles.at[:, pl.ds(cache_count_here - REACH, REACH), :, cols],
                    there.at[:, pl.ds(0, REACH)],
                    far_send.at[head, 0], far_recv.at[head, 0], (above, group),
                ),
                remote(
                    cache_tiles.at[:, pl.ds(0, REACH), :, cols],
                    there.at[:, pl.ds(REACH + cache_count_here, REACH)],
                    far_send.at[head, 1], far_recv.at[head, 1], (below, group),
                ),
            )
        )
        near.append(
            (
                remote(
                    new_qkv.at[pl.ds(1, 2), pl.ds(rows_here - TILE, TILE), cols],
                    edge.at[:, pl.ds(0, TILE)],
                    near_send.at[head, 0], near_recv.at[head, 0], (above, group),
                ),
                remote(
                    new_qkv.at[pl.ds(1, 2), pl.ds(0, TILE), cols],
                    edge.at[:, pl.ds(TILE + rows_here, TILE)],
                    near_send.at[head, 1], near_recv.at[head, 1], (below, group),
                ),
            )
        )

    for head in range(EARLY):
        for copy in far[head]:
            copy.start()

    held = []
    for head, (chunk, at) in enumerate(place):
        cols = columns(head)
        held.append(
            (
                local(
                    cache_tiles.at[:, :, :, cols],
                    caches[chunk].at[at, :, pl.ds(REACH, cache_count_here)],
                    local_sem.at[head, 0],
                ),
                local(
                    new_qkv.at[2, :, cols],
                    news[chunk].at[at, 1, pl.ds(TILE, rows_here)],
                    local_sem.at[head, 1],
                ),
            )
        )

    sums[...] = jnp.zeros_like(sums)
    for t in range(tiles):
        raw_copies[t].wait()
        for which in range(2):
            total = jnp.zeros((TILE, HEAD_DIM), jnp.float32)
            for head in range(heads):
                wide = raw[which, pl.ds(t * TILE, TILE), columns(head)].astype(jnp.float32)
                total += wide * wide
            sums[pl.ds(8 * which + t, 1), :] = jnp.sum(total.T, axis=0, keepdims=True)
    sum_copies = [
        remote(sums, peer_sums.at[i], sum_send.at[i], sum_recv.at[i], (row, peer))
        for i, peer in enumerate(peers)
    ]
    for copy in sum_copies:
        copy.start()
    for copy in sum_copies:
        copy.wait_recv()
    square = sums[...]
    for i in range(len(peers)):
        square += peer_sums[i]
    rates[...] = lax.rsqrt(square / (width * n_groups) + 1e-06)
    rate_copies = [
        remote(
            rates.at[pl.ds(8, 8)], halo_rates.at[side], rate_send.at[side], rate_recv.at[side],
            (device, group),
        )
        for side, device in enumerate((above, below))
    ]
    for copy in rate_copies:
        copy.start()
    for head in range(EARLY):
        for copy in near[head]:
            copy.start()
    for head in range(EARLY, heads):
        for copy in far[head] + near[head]:
            copy.start()

    def spread(line):
        return jnp.broadcast_to(line, (TILE, TILE)).T

    for t in range(tiles):
        q_scale[t] = spread(rates[pl.ds(t, 1), :])
        k_scale[t] = spread(rates[pl.ds(8 + t, 1), :])

    dead = jnp.full((1, TILE), -jnp.inf, jnp.float32)
    lowest_new = row * tiles
    for t in range(tiles):
        live = {i: jnp.zeros((1, TILE), jnp.int32) for i in (0, 2)}
        count = jnp.full((1, TILE), new_count[t], jnp.int32)
        for j in range(1, new_list.shape[0]):
            tile = jnp.full((1, TILE), new_list[j, t], jnp.int32) - (lowest_new + t)
            for i in live:
                live[i] = jnp.where((tile == i - 1) & (count > j), 1, live[i])
        count = jnp.full((1, TILE), cache_count[t], jnp.int32)
        for j in range(1, cache_list.shape[1]):
            live[3 + j] = jnp.where(count > j, 1, 0)
        for i, line in live.items():
            bias[t, i : i + 1, :] = jnp.where(line > 0, jnp.float32(0), dead)

    lowest_cache = row * cache_count_here - REACH
    power = HEAD_DIM ** (-0.5) * 1.4426950408889634

    def attend(chunk, at, head, t):
        start = pl.multiple_of(t * TILE, TILE)
        cols = pl.ds(pl.multiple_of(head * HEAD_DIM, HEAD_DIM), HEAD_DIM)
        near_rows = pl.ds(start, 3 * TILE)
        query = raw[0, pl.ds(start, TILE), cols].astype(jnp.float32)
        query = (query * q_scale[t] * q_gain[cols]).astype(jnp.bfloat16)
        far_tiles = [
            jnp.clip(cache_list[t, j] - lowest_cache, 0, cache_count_here + 2 * REACH - 1)
            for j in range(cache_list.shape[1])
        ]
        keys = [news[chunk][at, 0, near_rows, :]] + [caches[chunk][at, 0, i] for i in far_tiles]
        values = [news[chunk][at, 1, near_rows, :]] + [caches[chunk][at, 1, i] for i in far_tiles]
        scores = lax.dot_general(
            query, jnp.concatenate(keys, axis=0), (((1,), (1,)), ((), ())),
            preferred_element_type=jnp.float32,
        )
        parts = []
        for i in range(3 + len(far_tiles)):
            part = scores[:, i * TILE : (i + 1) * TILE]
            parts.append(part if i in (1, 3) else part + bias[t, i : i + 1, :])
        top = functools.reduce(jnp.maximum, parts)
        top = jnp.max(top, axis=1, keepdims=True)
        weights = [jnp.exp2((part - top) * power) for part in parts]
        total = jnp.sum(functools.reduce(jnp.add, weights), axis=1, keepdims=True)
        weights = jnp.concatenate([w.astype(jnp.bfloat16) for w in weights], axis=1)
        result = jnp.dot(
            weights, jnp.concatenate(values, axis=0), preferred_element_type=jnp.float32
        )
        mixed[head, pl.ds(start, TILE), :] = (result / total).astype(jnp.bfloat16)

    def normed_keys(chunk, at, head, t, scale):
        cols = pl.ds(pl.multiple_of(head * HEAD_DIM, HEAD_DIM), HEAD_DIM)
        wide = raw[1, pl.ds(pl.multiple_of(t * TILE, TILE), TILE), cols].astype(jnp.float32)
        return (wide * scale * k_gain[cols]).astype(jnp.bfloat16)

    out_copies = []
    first = 0
    for chunk, count in enumerate(CHUNKS):
        for head in range(first, first + count):
            for copy in held[head]:
                copy.wait()
            for copy in far[head]:
                copy.wait_recv()

        @pl.loop(0, count)
        def inner(at):
            head = first + at

            @pl.loop(0, tiles)
            def norm(t):
                news[chunk][at, 0, pl.ds(pl.multiple_of((t + 1) * TILE, TILE), TILE), :] = (
                    normed_keys(chunk, at, head, t, k_scale[t])
                )

            @pl.loop(1, tiles - 1)
            def middle(t):
                attend(chunk, at, head, t)

        if chunk == 0:
            for copy in rate_copies:
                copy.wait_recv()
            halo_scale[0] = spread(halo_rates[0, pl.ds(tiles - 1, 1), :])
            halo_scale[1] = spread(halo_rates[1, pl.ds(0, 1), :])
        for head in range(first, first + count):
            for copy in near[head]:
                copy.wait_recv()

        @pl.loop(0, count)
        def edges(at):
            head = first + at
            cols = pl.ds(pl.multiple_of(head * HEAD_DIM, HEAD_DIM), HEAD_DIM)
            for side in range(2):
                where = pl.ds(side * (TILE + rows_here), TILE)
                wide = news[chunk][at, 0, where, :].astype(jnp.float32)
                news[chunk][at, 0, where, :] = (wide * halo_scale[side] * k_gain[cols]).astype(
                    jnp.bfloat16
                )

            @pl.loop(0, 2)
            def ends(side):
                attend(chunk, at, head, side * (tiles - 1))

        for head in range(first, first + count):
            out_copies.append(local(mixed.at[head], out.at[:, columns(head)], out_sem.at[head]))
        first += count

    for copy in out_copies:
        copy.wait()
    for copy in sum_copies + rate_copies:
        copy.wait_send()
    for pair in far + near:
        for copy in pair:
            copy.wait_send()


def on_device(new_qkv, cache_kv, q_gain, k_gain, new_list, new_count, cache_list, cache_count):
    rows_here, width = new_qkv.shape[1:]
    cache_rows = cache_kv.shape[1]
    tiles = rows_here // TILE
    heads = width // HEAD_DIM
    groups = lax.axis_size("heads")
    in_smem = pl.BlockSpec(memory_space=pltpu.SMEM)
    in_vmem = pl.BlockSpec(memory_space=pltpu.VMEM)
    anywhere = pl.BlockSpec(memory_space=pl.ANY)
    dma = pltpu.SemaphoreType.DMA
    keys_here = (tiles + 3 + cache_list.shape[1]) * TILE
    return pl.pallas_call(
        kernel,
        out_shape=jax.ShapeDtypeStruct((rows_here, width), jnp.bfloat16),
        in_specs=[in_smem] * 4 + [in_vmem] * 2 + [anywhere] * 2,
        out_specs=anywhere,
        scratch_shapes=[
            pltpu.VMEM((count, 2, rows_here + 2 * TILE, HEAD_DIM), jnp.bfloat16)
            for count in CHUNKS
        ]
        + [
            pltpu.VMEM((count, 2, cache_rows // TILE + 2 * REACH, TILE, HEAD_DIM), jnp.bfloat16)
            for count in CHUNKS
        ]
        + [
            pltpu.VMEM((2, rows_here, width), jnp.bfloat16),
            pltpu.VMEM((tiles, TILE, HEAD_DIM), jnp.float32),
            pltpu.VMEM((tiles, TILE, HEAD_DIM), jnp.float32),
            pltpu.VMEM((2, TILE, HEAD_DIM), jnp.float32),
            pltpu.VMEM((16, TILE), jnp.float32),
            pltpu.VMEM((groups - 1, 16, TILE), jnp.float32),
            pltpu.VMEM((16, TILE), jnp.float32),
            pltpu.VMEM((2, 8, TILE), jnp.float32),
            pltpu.VMEM((tiles, 3 + cache_list.shape[1], TILE), jnp.float32),
            pltpu.VMEM((heads, rows_here, HEAD_DIM), jnp.bfloat16),
            dma((tiles,)),
            dma((heads, 2)),
            dma((heads, 2)),
            dma((heads, 2)),
            dma((heads, 2)),
            dma((heads, 2)),
            dma((groups - 1,)),
            dma((groups - 1,)),
            dma((2,)),
            dma((2,)),
            dma((heads,)),
        ],
        compiler_params=pltpu.CompilerParams(
            collective_id=0, has_side_effects=True, vmem_limit_bytes=56 * 2**20
        ),
        cost_estimate=pl.CostEstimate(
            flops=4 * rows_here * keys_here * width,
            bytes_accessed=2 * (4 * rows_here + 2 * cache_rows) * width,
            transcendentals=rows_here * keys_here * heads,
        ),
    )(
        new_list.T,
        new_count,
        cache_list,
        cache_count,
        q_gain,
        k_gain,
        new_qkv,
        cache_kv.reshape(2, cache_rows // TILE, TILE, width),
    )


def solution(mesh):
    placed = (
        P(None, "rows", "heads"),
        P(None, "rows", "heads"),
        P("heads"),
        P("heads"),
        P("rows", None),
        P("rows"),
        P("rows", None),
        P("rows"),
    )
    return jax.shard_map(
        on_device, mesh=mesh, in_specs=placed, out_specs=P("rows", "heads"), check_vma=False
    )
```

```python
import functools

import jax
import jax.numpy as jnp
from jax import lax
from jax.experimental import pallas as pl
from jax.experimental.pallas import tpu as pltpu
from jax.sharding import PartitionSpec as P

HEADS = 40
HEAD_DIM = 128
TILE = 128
REACH = 2
CHUNKS = (2, 2, 2, 2, 1, 1)
EARLY = 3
MESH = pl.DeviceIdType.MESH


def kernel(
    new_list, new_count, cache_list, cache_count, q_gain, k_gain, new_qkv, cache_tiles, out, *scratch
):
    n_chunks = len(CHUNKS)
    news, caches = scratch[:n_chunks], scratch[n_chunks : 2 * n_chunks]
    (raw, q_scale, k_scale, halo_scale, sums, peer_sums, rates, halo_rates, bias, mixed) = scratch[
        2 * n_chunks : 2 * n_chunks + 10
    ]
    (raw_sem, local_sem, far_send, far_recv, near_send, near_recv, sum_send, sum_recv,
     rate_send, rate_recv, out_sem) = scratch[2 * n_chunks + 10 :]
    row, group = lax.axis_index("rows"), lax.axis_index("heads")
    n_rows, n_groups = lax.axis_size("rows"), lax.axis_size("heads")
    above, below = lax.rem(row + 1, n_rows), lax.rem(row + n_rows - 1, n_rows)
    peers = [lax.rem(group + step, n_groups) for step in range(1, n_groups)]
    rows_here, width = new_qkv.shape[1:]
    cache_count_here = cache_tiles.shape[1]
    tiles = rows_here // TILE
    heads = width // HEAD_DIM
    bend = n_rows // 2
    place = [(chunk, at) for chunk, count in enumerate(CHUNKS) for at in range(count)]

    def columns(head):
        return pl.ds(head * HEAD_DIM, HEAD_DIM)

    def local(source, target, sem):
        copy = pltpu.make_async_copy(source, target, sem)
        copy.start()
        return copy

    def remote(source, target, send, recv, device):
        return pltpu.make_async_remote_copy(
            src_ref=source, dst_ref=target, send_sem=send, recv_sem=recv,
            device_id=device, device_id_type=MESH,
        )

    raw_copies = [
        local(
            new_qkv.at[pl.ds(0, 2), pl.ds(t * TILE, TILE)],
            raw.at[:, pl.ds(t * TILE, TILE)],
            raw_sem.at[t],
        )
        for t in range(tiles)
    ]

    barrier = pltpu.get_barrier_semaphore()
    for device in [(above, group), (below, group)] + [(row, peer) for peer in peers]:
        pl.semaphore_signal(barrier, inc=1, device_id=device, device_id_type=MESH)
    for ones, others in (((bend - 1, bend), (0, n_rows - 1)), ((0, n_rows - 1), (bend - 1, bend))):

        @pl.when((row == ones[0]) | (row == ones[1]))
        def greet():
            for other in others:
                pl.semaphore_signal(barrier, inc=1, device_id=(other, group), device_id_type=MESH)

    ends = (row == 0) | (row == n_rows - 1) | (row == bend - 1) | (row == bend)
    pl.semaphore_wait(barrier, jnp.where(ends, n_groups + 3, n_groups + 1))

    far, near = [], []

    def exchange(head, top, bottom, low, high, send, recv):
        over_last = head % 2 == 0
        middle, at_middle = (high, (n_rows - 1, group)) if over_last else (low, (0, group))
        side = int(over_last)
        return (
            remote(top, low, send.at[head, 0], recv.at[head, 0], (above, group)),
            remote(bottom, high, send.at[head, 1], recv.at[head, 1], (below, group)),
            remote(top, middle, send.at[head, 0], recv.at[head, side], at_middle),
            remote(middle, low, send.at[head, 1 - side], recv.at[head, 0], (bend, group)),
        )

    for head, (chunk, at) in enumerate(place):
        cols = columns(head)
        there, edge = caches[chunk].at[at], news[chunk].at[at]
        far.append(
            exchange(
                head,
                cache_tiles.at[:, pl.ds(cache_count_here - REACH, REACH), :, cols],
                cache_tiles.at[:, pl.ds(0, REACH), :, cols],
                there.at[:, pl.ds(0, REACH)],
                there.at[:, pl.ds(REACH + cache_count_here, REACH)],
                far_send,
                far_recv,
            )
        )
        near.append(
            exchange(
                head,
                new_qkv.at[pl.ds(1, 2), pl.ds(rows_here - TILE, TILE), cols],
                new_qkv.at[pl.ds(1, 2), pl.ds(0, TILE), cols],
                edge.at[:, pl.ds(0, TILE)],
                edge.at[:, pl.ds(TILE + rows_here, TILE)],
                near_send,
                near_recv,
            )
        )

    def start(ways):
        pl.when((row < n_rows - 1) & (row != bend - 1))(ways[0].start)
        pl.when(row == bend - 1)(ways[2].start)
        pl.when(row > 0)(ways[1].start)

    def arrive(ways):
        pl.when(row > 0)(ways[0].wait_recv)
        pl.when(row < n_rows - 1)(ways[1].wait_recv)

    def relay(pair):
        if 2 * pair >= heads:
            return

        @pl.when(row == n_rows - 1)
        def even():
            for ways in (far[2 * pair], near[2 * pair]):
                ways[1].wait_recv()
                ways[3].start()

        @pl.when(row == 0)
        def odd():
            for ways in (far[2 * pair + 1], near[2 * pair + 1]):
                ways[0].wait_recv()
                ways[3].start()

    for head in range(EARLY):
        start(far[head])

    def clear(head, line):
        chunk, at = place[head]
        news[chunk][at, :, pl.ds(line, TILE), :] = jnp.zeros((2, TILE, HEAD_DIM), jnp.bfloat16)

    @pl.when(row == 0)
    def none_below():
        for head in range(0, heads, 2):
            clear(head, 0)

    @pl.when(row == n_rows - 1)
    def none_above():
        for head in range(1, heads, 2):
            clear(head, TILE + rows_here)

    held = []
    for head, (chunk, at) in enumerate(place):
        cols = columns(head)
        held.append(
            (
                local(
                    cache_tiles.at[:, :, :, cols],
                    caches[chunk].at[at, :, pl.ds(REACH, cache_count_here)],
                    local_sem.at[head, 0],
                ),
                local(
                    new_qkv.at[2, :, cols],
                    news[chunk].at[at, 1, pl.ds(TILE, rows_here)],
                    local_sem.at[head, 1],
                ),
            )
        )

    sums[...] = jnp.zeros_like(sums)
    for t in range(tiles):
        raw_copies[t].wait()
        for which in range(2):
            total = jnp.zeros((TILE, HEAD_DIM), jnp.float32)
            for head in range(heads):
                wide = raw[which, pl.ds(t * TILE, TILE), columns(head)].astype(jnp.float32)
                total += wide * wide
            sums[pl.ds(8 * which + t, 1), :] = jnp.sum(total.T, axis=0, keepdims=True)
    sum_copies = [
        remote(sums, peer_sums.at[i], sum_send.at[i], sum_recv.at[i], (row, peer))
        for i, peer in enumerate(peers)
    ]
    for copy in sum_copies:
        copy.start()
    for copy in sum_copies:
        copy.wait_recv()
    square = sums[...]
    for i in range(len(peers)):
        square += peer_sums[i]
    rates[...] = lax.rsqrt(square / (width * n_groups) + 1e-06)
    rate_copies = [
        remote(
            rates.at[pl.ds(8, 8)], halo_rates.at[side], rate_send.at[side], rate_recv.at[side],
            (device, group),
        )
        for side, device in enumerate((above, below))
    ]
    for copy in rate_copies:
        copy.start()
    for head in range(EARLY):
        start(near[head])
    for head in range(EARLY, heads):
        start(far[head])
        start(near[head])

    def spread(line):
        return jnp.broadcast_to(line, (TILE, TILE)).T

    for t in range(tiles):
        q_scale[t] = spread(rates[pl.ds(t, 1), :])
        k_scale[t] = spread(rates[pl.ds(8 + t, 1), :])

    dead = jnp.full((1, TILE), -jnp.inf, jnp.float32)
    lowest_new = row * tiles
    for t in range(tiles):
        live = {i: jnp.zeros((1, TILE), jnp.int32) for i in (0, 2)}
        count = jnp.full((1, TILE), new_count[t], jnp.int32)
        for j in range(1, new_list.shape[0]):
            tile = jnp.full((1, TILE), new_list[j, t], jnp.int32) - (lowest_new + t)
            for i in live:
                live[i] = jnp.where((tile == i - 1) & (count > j), 1, live[i])
        count = jnp.full((1, TILE), cache_count[t], jnp.int32)
        for j in range(1, cache_list.shape[1]):
            live[3 + j] = jnp.where(count > j, 1, 0)
        for i, line in live.items():
            bias[t, i : i + 1, :] = jnp.where(line > 0, jnp.float32(0), dead)

    lowest_cache = row * cache_count_here - REACH
    power = HEAD_DIM ** (-0.5) * 1.4426950408889634

    def attend(chunk, at, head, t):
        start = t * TILE
        cols = pl.ds(pl.multiple_of(head * HEAD_DIM, HEAD_DIM), HEAD_DIM)
        near_rows = pl.ds(start, 3 * TILE)
        query = raw[0, pl.ds(start, TILE), cols].astype(jnp.float32)
        query = (query * q_scale[t] * q_gain[cols]).astype(jnp.bfloat16)
        far_tiles = [
            jnp.clip(cache_list[t, j] - lowest_cache, 0, cache_count_here + 2 * REACH - 1)
            for j in range(cache_list.shape[1])
        ]
        keys = [news[chunk][at, 0, near_rows, :]] + [caches[chunk][at, 0, i] for i in far_tiles]
        values = [news[chunk][at, 1, near_rows, :]] + [caches[chunk][at, 1, i] for i in far_tiles]
        scores = lax.dot_general(
            query, jnp.concatenate(keys, axis=0), (((1,), (1,)), ((), ())),
            preferred_element_type=jnp.float32,
        )
        parts = []
        for i in range(3 + len(far_tiles)):
            part = scores[:, i * TILE : (i + 1) * TILE]
            parts.append(part if i in (1, 3) else part + bias[t, i : i + 1, :])
        top = functools.reduce(jnp.maximum, parts)
        top = jnp.max(top, axis=1, keepdims=True)
        weights = [jnp.exp2((part - top) * power) for part in parts]
        total = jnp.sum(functools.reduce(jnp.add, weights), axis=1, keepdims=True)
        weights = jnp.concatenate([w.astype(jnp.bfloat16) for w in weights], axis=1)
        result = jnp.dot(
            weights, jnp.concatenate(values, axis=0), preferred_element_type=jnp.float32
        )
        mixed[head, pl.ds(start, TILE), :] = (result / total).astype(jnp.bfloat16)

    def normed_keys(head, t):
        cols = pl.ds(pl.multiple_of(head * HEAD_DIM, HEAD_DIM), HEAD_DIM)
        wide = raw[1, pl.ds(t * TILE, TILE), cols].astype(jnp.float32)
        return (wide * k_scale[t] * k_gain[cols]).astype(jnp.bfloat16)

    out_copies = []
    first = 0
    for chunk, count in enumerate(CHUNKS):
        for head in range(first, first + count):
            for copy in held[head]:
                copy.wait()
            arrive(far[head])
        relay(2 * chunk)

        @pl.loop(0, count)
        def inner(at):
            head = first + at

            for t in range(tiles):
                news[chunk][at, 0, pl.ds((t + 1) * TILE, TILE), :] = normed_keys(head, t)

            for t in range(1, tiles - 1):
                attend(chunk, at, head, t)

        if chunk == 0:
            for copy in rate_copies:
                copy.wait_recv()
            halo_scale[0] = spread(halo_rates[0, pl.ds(tiles - 1, 1), :])
            halo_scale[1] = spread(halo_rates[1, pl.ds(0, 1), :])
        for head in range(first, first + count):
            arrive(near[head])
        relay(2 * chunk + 1)

        @pl.loop(0, count)
        def edges(at):
            head = first + at
            cols = pl.ds(pl.multiple_of(head * HEAD_DIM, HEAD_DIM), HEAD_DIM)

            def norm_halo(side):
                where = pl.ds(side * (TILE + rows_here), TILE)
                wide = news[chunk][at, 0, where, :].astype(jnp.float32)
                news[chunk][at, 0, where, :] = (wide * halo_scale[side] * k_gain[cols]).astype(
                    jnp.bfloat16
                )

            pl.when(row > 0)(lambda: norm_halo(0))
            pl.when(row < n_rows - 1)(lambda: norm_halo(1))

            for t in (0, tiles - 1):
                attend(chunk, at, head, t)

        for head in range(first, first + count):
            out_copies.append(local(mixed.at[head], out.at[:, columns(head)], out_sem.at[head]))
        first += count

    for copy in out_copies:
        copy.wait()
    for copy in sum_copies + rate_copies:
        copy.wait_send()
    for head in range(heads):
        for ways in (far[head], near[head]):
            if head % 2 == 0:
                ways[0].wait_send()
                pl.when(row > 0)(ways[1].wait_send)
            else:
                pl.when(row < n_rows - 1)(ways[0].wait_send)
                ways[1].wait_send()


def on_device(new_qkv, cache_kv, q_gain, k_gain, new_list, new_count, cache_list, cache_count):
    rows_here, width = new_qkv.shape[1:]
    cache_rows = cache_kv.shape[1]
    tiles = rows_here // TILE
    heads = width // HEAD_DIM
    groups = lax.axis_size("heads")
    in_smem = pl.BlockSpec(memory_space=pltpu.SMEM)
    in_vmem = pl.BlockSpec(memory_space=pltpu.VMEM)
    anywhere = pl.BlockSpec(memory_space=pl.ANY)
    dma = pltpu.SemaphoreType.DMA
    keys_here = (tiles + 3 + cache_list.shape[1]) * TILE
    return pl.pallas_call(
        kernel,
        out_shape=jax.ShapeDtypeStruct((rows_here, width), jnp.bfloat16),
        in_specs=[in_smem] * 4 + [in_vmem] * 2 + [anywhere] * 2,
        out_specs=anywhere,
        scratch_shapes=[
            pltpu.VMEM((count, 2, rows_here + 2 * TILE, HEAD_DIM), jnp.bfloat16)
            for count in CHUNKS
        ]
        + [
            pltpu.VMEM((count, 2, cache_rows // TILE + 2 * REACH, TILE, HEAD_DIM), jnp.bfloat16)
            for count in CHUNKS
        ]
        + [
            pltpu.VMEM((2, rows_here, width), jnp.bfloat16),
            pltpu.VMEM((tiles, TILE, HEAD_DIM), jnp.float32),
            pltpu.VMEM((tiles, TILE, HEAD_DIM), jnp.float32),
            pltpu.VMEM((2, TILE, HEAD_DIM), jnp.float32),
            pltpu.VMEM((16, TILE), jnp.float32),
            pltpu.VMEM((groups - 1, 16, TILE), jnp.float32),
            pltpu.VMEM((16, TILE), jnp.float32),
            pltpu.VMEM((2, 8, TILE), jnp.float32),
            pltpu.VMEM((tiles, 3 + cache_list.shape[1], TILE), jnp.float32),
            pltpu.VMEM((heads, rows_here, HEAD_DIM), jnp.bfloat16),
            dma((tiles,)),
            dma((heads, 2)),
            dma((heads, 2)),
            dma((heads, 2)),
            dma((heads, 2)),
            dma((heads, 2)),
            dma((groups - 1,)),
            dma((groups - 1,)),
            dma((2,)),
            dma((2,)),
            dma((heads,)),
        ],
        compiler_params=pltpu.CompilerParams(
            collective_id=0, has_side_effects=True, vmem_limit_bytes=56 * 2**20
        ),
        cost_estimate=pl.CostEstimate(
            flops=4 * rows_here * keys_here * width,
            bytes_accessed=2 * (4 * rows_here + 2 * cache_rows) * width,
            transcendentals=rows_here * keys_here * heads,
        ),
    )(
        new_list.T,
        new_count,
        cache_list,
        cache_count,
        q_gain,
        k_gain,
        new_qkv,
        cache_kv.reshape(2, cache_rows // TILE, TILE, width),
    )


def solution(mesh):
    placed = (
        P(None, "rows", "heads"),
        P(None, "rows", "heads"),
        P("heads"),
        P("heads"),
        P("rows", None),
        P("rows"),
        P("rows", None),
        P("rows"),
    )
    return jax.shard_map(
        on_device, mesh=mesh, in_specs=placed, out_specs=P("rows", "heads"), check_vma=False
    )
```

```python
import functools

import jax
import jax.numpy as jnp
from jax import lax
from jax.experimental import pallas as pl
from jax.experimental.pallas import tpu as pltpu
from jax.sharding import PartitionSpec as P

HEADS = 40
HEAD_DIM = 128
TILE = 128
REACH = 2
CHUNKS = (2, 2, 2, 2, 1, 1)
EARLY = 3
MESH = pl.DeviceIdType.MESH


def kernel(
    new_list, new_count, cache_list, cache_count, q_gain, k_gain, new_qkv, cache_tiles, out, *scratch
):
    n_chunks = len(CHUNKS)
    news, caches = scratch[:n_chunks], scratch[n_chunks : 2 * n_chunks]
    (raw, q_scale, k_scale, halo_scale, sums, peer_sums, rates, halo_rates, bias) = scratch[
        2 * n_chunks : 2 * n_chunks + 9
    ]
    (raw_sem, local_sem, far_send, far_recv, near_send, near_recv, sum_send, sum_recv,
     rate_send, rate_recv) = scratch[2 * n_chunks + 9 :]
    row, group = lax.axis_index("rows"), lax.axis_index("heads")
    n_rows, n_groups = lax.axis_size("rows"), lax.axis_size("heads")
    above, below = lax.rem(row + 1, n_rows), lax.rem(row + n_rows - 1, n_rows)
    peers = [lax.rem(group + step, n_groups) for step in range(1, n_groups)]
    rows_here, width = new_qkv.shape[1:]
    cache_count_here = cache_tiles.shape[1]
    tiles = rows_here // TILE
    heads = width // HEAD_DIM
    bend = n_rows // 2
    place = [(chunk, at) for chunk, count in enumerate(CHUNKS) for at in range(count)]

    def columns(head):
        return pl.ds(head * HEAD_DIM, HEAD_DIM)

    def local(source, target, sem):
        copy = pltpu.make_async_copy(source, target, sem)
        copy.start()
        return copy

    def remote(source, target, send, recv, device):
        return pltpu.make_async_remote_copy(
            src_ref=source, dst_ref=target, send_sem=send, recv_sem=recv,
            device_id=device, device_id_type=MESH,
        )

    raw_copies = [
        local(
            new_qkv.at[pl.ds(0, 2), pl.ds(t * TILE, TILE)],
            raw.at[:, pl.ds(t * TILE, TILE)],
            raw_sem.at[t],
        )
        for t in range(tiles)
    ]

    barrier = pltpu.get_barrier_semaphore()
    for device in [(above, group), (below, group)] + [(row, peer) for peer in peers]:
        pl.semaphore_signal(barrier, inc=1, device_id=device, device_id_type=MESH)
    for ones, others in (((bend - 1, bend), (0, n_rows - 1)), ((0, n_rows - 1), (bend - 1, bend))):

        @pl.when((row == ones[0]) | (row == ones[1]))
        def greet():
            for other in others:
                pl.semaphore_signal(barrier, inc=1, device_id=(other, group), device_id_type=MESH)

    ends = (row == 0) | (row == n_rows - 1) | (row == bend - 1) | (row == bend)
    pl.semaphore_wait(barrier, jnp.where(ends, n_groups + 3, n_groups + 1))

    far, near = [], []

    def exchange(head, top, bottom, low, high, send, recv):
        over_last = head % 2 == 0
        middle, at_middle = (high, (n_rows - 1, group)) if over_last else (low, (0, group))
        side = int(over_last)
        return (
            remote(top, low, send.at[head, 0], recv.at[head, 0], (above, group)),
            remote(bottom, high, send.at[head, 1], recv.at[head, 1], (below, group)),
            remote(top, middle, send.at[head, 0], recv.at[head, side], at_middle),
            remote(middle, low, send.at[head, 1 - side], recv.at[head, 0], (bend, group)),
        )

    for head, (chunk, at) in enumerate(place):
        cols = columns(head)
        there, edge = caches[chunk].at[at], news[chunk].at[at]
        far.append(
            exchange(
                head,
                cache_tiles.at[:, pl.ds(cache_count_here - REACH, REACH), :, cols],
                cache_tiles.at[:, pl.ds(0, REACH), :, cols],
                there.at[:, pl.ds(0, REACH)],
                there.at[:, pl.ds(REACH + cache_count_here, REACH)],
                far_send,
                far_recv,
            )
        )
        near.append(
            exchange(
                head,
                new_qkv.at[pl.ds(1, 2), pl.ds(rows_here - TILE, TILE), cols],
                new_qkv.at[pl.ds(1, 2), pl.ds(0, TILE), cols],
                edge.at[:, pl.ds(0, TILE)],
                edge.at[:, pl.ds(TILE + rows_here, TILE)],
                near_send,
                near_recv,
            )
        )

    def start(ways):
        pl.when((row < n_rows - 1) & (row != bend - 1))(ways[0].start)
        pl.when(row == bend - 1)(ways[2].start)
        pl.when(row > 0)(ways[1].start)

    def arrive(ways):
        pl.when(row > 0)(ways[0].wait_recv)
        pl.when(row < n_rows - 1)(ways[1].wait_recv)

    def relay(pair):
        if 2 * pair >= heads:
            return

        @pl.when(row == n_rows - 1)
        def even():
            for ways in (far[2 * pair], near[2 * pair]):
                ways[1].wait_recv()
                ways[3].start()

        @pl.when(row == 0)
        def odd():
            for ways in (far[2 * pair + 1], near[2 * pair + 1]):
                ways[0].wait_recv()
                ways[3].start()

    for head in range(EARLY):
        start(far[head])

    def clear(head, line):
        chunk, at = place[head]
        news[chunk][at, :, pl.ds(line, TILE), :] = jnp.zeros((2, TILE, HEAD_DIM), jnp.bfloat16)

    @pl.when(row == 0)
    def none_below():
        for head in range(0, heads, 2):
            clear(head, 0)

    @pl.when(row == n_rows - 1)
    def none_above():
        for head in range(1, heads, 2):
            clear(head, TILE + rows_here)

    held = []
    for head, (chunk, at) in enumerate(place):
        cols = columns(head)
        held.append(
            (
                local(
                    cache_tiles.at[:, :, :, cols],
                    caches[chunk].at[at, :, pl.ds(REACH, cache_count_here)],
                    local_sem.at[head, 0],
                ),
                local(
                    new_qkv.at[2, :, cols],
                    news[chunk].at[at, 1, pl.ds(TILE, rows_here)],
                    local_sem.at[head, 1],
                ),
            )
        )

    sums[...] = jnp.zeros_like(sums)
    for t in range(tiles):
        raw_copies[t].wait()
        for which in range(2):
            total = jnp.zeros((TILE, HEAD_DIM), jnp.float32)
            for head in range(heads):
                wide = raw[which, pl.ds(t * TILE, TILE), columns(head)].astype(jnp.float32)
                total += wide * wide
            sums[pl.ds(8 * which + t, 1), :] = jnp.sum(total.T, axis=0, keepdims=True)
    sum_copies = [
        remote(sums, peer_sums.at[i], sum_send.at[i], sum_recv.at[i], (row, peer))
        for i, peer in enumerate(peers)
    ]
    for copy in sum_copies:
        copy.start()
    for copy in sum_copies:
        copy.wait_recv()
    square = sums[...]
    for i in range(len(peers)):
        square += peer_sums[i]
    rates[...] = lax.rsqrt(square / (width * n_groups) + 1e-06)
    rate_copies = [
        remote(
            rates.at[pl.ds(8, 8)], halo_rates.at[side], rate_send.at[side], rate_recv.at[side],
            (device, group),
        )
        for side, device in enumerate((above, below))
    ]
    for copy in rate_copies:
        copy.start()
    for head in range(EARLY):
        start(near[head])
    for head in range(EARLY, heads):
        start(far[head])
        start(near[head])

    def spread(line):
        return jnp.broadcast_to(line, (TILE, TILE)).T

    for t in range(tiles):
        q_scale[t] = spread(rates[pl.ds(t, 1), :])
        k_scale[t] = spread(rates[pl.ds(8 + t, 1), :])

    dead = jnp.full((1, TILE), -jnp.inf, jnp.float32)
    lowest_new = row * tiles
    for t in range(tiles):
        live = {i: jnp.zeros((1, TILE), jnp.int32) for i in (0, 2)}
        count = jnp.full((1, TILE), new_count[t], jnp.int32)
        for j in range(1, new_list.shape[0]):
            tile = jnp.full((1, TILE), new_list[j, t], jnp.int32) - (lowest_new + t)
            for i in live:
                live[i] = jnp.where((tile == i - 1) & (count > j), 1, live[i])
        count = jnp.full((1, TILE), cache_count[t], jnp.int32)
        for j in range(1, cache_list.shape[1]):
            live[3 + j] = jnp.where(count > j, 1, 0)
        for i, line in live.items():
            bias[t, i : i + 1, :] = jnp.where(line > 0, jnp.float32(0), dead)

    lowest_cache = row * cache_count_here - REACH
    power = HEAD_DIM ** (-0.5) * 1.4426950408889634

    def attend(chunk, at, head, t):
        start = t * TILE
        cols = pl.ds(pl.multiple_of(head * HEAD_DIM, HEAD_DIM), HEAD_DIM)
        near_rows = pl.ds(start, 3 * TILE)
        query = raw[0, pl.ds(start, TILE), cols].astype(jnp.float32)
        query = (query * q_scale[t] * q_gain[cols]).astype(jnp.bfloat16)
        far_tiles = [
            jnp.clip(cache_list[t, j] - lowest_cache, 0, cache_count_here + 2 * REACH - 1)
            for j in range(cache_list.shape[1])
        ]
        keys = [news[chunk][at, 0, near_rows, :]] + [caches[chunk][at, 0, i] for i in far_tiles]
        values = [news[chunk][at, 1, near_rows, :]] + [caches[chunk][at, 1, i] for i in far_tiles]
        scores = lax.dot_general(
            query, jnp.concatenate(keys, axis=0), (((1,), (1,)), ((), ())),
            preferred_element_type=jnp.float32,
        )
        parts = []
        for i in range(3 + len(far_tiles)):
            part = scores[:, i * TILE : (i + 1) * TILE]
            parts.append(part if i in (1, 3) else part + bias[t, i : i + 1, :])
        top = functools.reduce(jnp.maximum, parts)
        top = jnp.max(top, axis=1, keepdims=True)
        weights = [jnp.exp2((part - top) * power) for part in parts]
        total = jnp.sum(functools.reduce(jnp.add, weights), axis=1, keepdims=True)
        weights = jnp.concatenate([w.astype(jnp.bfloat16) for w in weights], axis=1)
        result = jnp.dot(
            weights, jnp.concatenate(values, axis=0), preferred_element_type=jnp.float32
        )
        out[pl.ds(start, TILE), cols] = (result / total).astype(jnp.bfloat16)

    def normed_keys(head, t):
        cols = pl.ds(pl.multiple_of(head * HEAD_DIM, HEAD_DIM), HEAD_DIM)
        wide = raw[1, pl.ds(t * TILE, TILE), cols].astype(jnp.float32)
        return (wide * k_scale[t] * k_gain[cols]).astype(jnp.bfloat16)

    first = 0
    for chunk, count in enumerate(CHUNKS):
        for head in range(first, first + count):
            for copy in held[head]:
                copy.wait()
            arrive(far[head])
        relay(2 * chunk)

        @pl.loop(0, count)
        def inner(at):
            head = first + at

            for t in range(tiles):
                news[chunk][at, 0, pl.ds((t + 1) * TILE, TILE), :] = normed_keys(head, t)

            for t in range(1, tiles - 1):
                attend(chunk, at, head, t)

        if chunk == 0:
            for copy in rate_copies:
                copy.wait_recv()
            halo_scale[0] = spread(halo_rates[0, pl.ds(tiles - 1, 1), :])
            halo_scale[1] = spread(halo_rates[1, pl.ds(0, 1), :])
        for head in range(first, first + count):
            arrive(near[head])
        relay(2 * chunk + 1)

        @pl.loop(0, count)
        def edges(at):
            head = first + at
            cols = pl.ds(pl.multiple_of(head * HEAD_DIM, HEAD_DIM), HEAD_DIM)

            def norm_halo(side):
                where = pl.ds(side * (TILE + rows_here), TILE)
                wide = news[chunk][at, 0, where, :].astype(jnp.float32)
                news[chunk][at, 0, where, :] = (wide * halo_scale[side] * k_gain[cols]).astype(
                    jnp.bfloat16
                )

            pl.when(row > 0)(lambda: norm_halo(0))
            pl.when(row < n_rows - 1)(lambda: norm_halo(1))

            for t in (0, tiles - 1):
                attend(chunk, at, head, t)

        first += count

    for copy in sum_copies + rate_copies:
        copy.wait_send()
    for head in range(heads):
        for ways in (far[head], near[head]):
            if head % 2 == 0:
                ways[0].wait_send()
                pl.when(row > 0)(ways[1].wait_send)
            else:
                pl.when(row < n_rows - 1)(ways[0].wait_send)
                ways[1].wait_send()


def on_device(new_qkv, cache_kv, q_gain, k_gain, new_list, new_count, cache_list, cache_count):
    rows_here, width = new_qkv.shape[1:]
    cache_rows = cache_kv.shape[1]
    tiles = rows_here // TILE
    heads = width // HEAD_DIM
    groups = lax.axis_size("heads")
    in_smem = pl.BlockSpec(memory_space=pltpu.SMEM)
    in_vmem = pl.BlockSpec(memory_space=pltpu.VMEM)
    anywhere = pl.BlockSpec(memory_space=pl.ANY)
    dma = pltpu.SemaphoreType.DMA
    keys_here = (tiles + 3 + cache_list.shape[1]) * TILE
    return pl.pallas_call(
        kernel,
        out_shape=pltpu.VMEM((rows_here, width), jnp.bfloat16),
        in_specs=[in_smem] * 4 + [in_vmem] * 2 + [anywhere] * 2,
        out_specs=in_vmem,
        scratch_shapes=[
            pltpu.VMEM((count, 2, rows_here + 2 * TILE, HEAD_DIM), jnp.bfloat16)
            for count in CHUNKS
        ]
        + [
            pltpu.VMEM((count, 2, cache_rows // TILE + 2 * REACH, TILE, HEAD_DIM), jnp.bfloat16)
            for count in CHUNKS
        ]
        + [
            pltpu.VMEM((2, rows_here, width), jnp.bfloat16),
            pltpu.VMEM((tiles, TILE, HEAD_DIM), jnp.float32),
            pltpu.VMEM((tiles, TILE, HEAD_DIM), jnp.float32),
            pltpu.VMEM((2, TILE, HEAD_DIM), jnp.float32),
            pltpu.VMEM((16, TILE), jnp.float32),
            pltpu.VMEM((groups - 1, 16, TILE), jnp.float32),
            pltpu.VMEM((16, TILE), jnp.float32),
            pltpu.VMEM((2, 8, TILE), jnp.float32),
            pltpu.VMEM((tiles, 3 + cache_list.shape[1], TILE), jnp.float32),
            dma((tiles,)),
            dma((heads, 2)),
            dma((heads, 2)),
            dma((heads, 2)),
            dma((heads, 2)),
            dma((heads, 2)),
            dma((groups - 1,)),
            dma((groups - 1,)),
            dma((2,)),
            dma((2,)),
        ],
        compiler_params=pltpu.CompilerParams(
            collective_id=0, has_side_effects=True, vmem_limit_bytes=60 * 2**20
        ),
        cost_estimate=pl.CostEstimate(
            flops=4 * rows_here * keys_here * width,
            bytes_accessed=2 * (4 * rows_here + 2 * cache_rows) * width,
            transcendentals=rows_here * keys_here * heads,
        ),
    )(
        new_list.T,
        new_count,
        cache_list,
        cache_count,
        q_gain,
        k_gain,
        new_qkv,
        cache_kv.reshape(2, cache_rows // TILE, TILE, width),
    )


def solution(mesh):
    placed = (
        P(None, "rows", "heads"),
        P(None, "rows", "heads"),
        P("heads"),
        P("heads"),
        P("rows", None),
        P("rows"),
        P("rows", None),
        P("rows"),
    )
    return jax.shard_map(
        on_device, mesh=mesh, in_specs=placed, out_specs=P("rows", "heads"), check_vma=False
    )
```

```python
import functools

import jax
import jax.numpy as jnp
from jax import lax
from jax.experimental import pallas as pl
from jax.experimental.pallas import tpu as pltpu
from jax.sharding import PartitionSpec as P

HEADS = 40
HEAD_DIM = 128
TILE = 128
REACH = 2
CHUNKS = (2, 2, 2, 1, 1, 1, 1)
LATE = 3
EARLY = 3
MESH = pl.DeviceIdType.MESH


def kernel(
    new_list, new_count, cache_list, cache_count, q_gain, k_gain, new_qkv, cache_tiles, out, *scratch
):
    n_chunks = len(CHUNKS)
    news, caches = scratch[:n_chunks], scratch[n_chunks : 2 * n_chunks]
    (raw, q_scale, k_scale, halo_scale, sums, peer_sums, rates, halo_rates, bias) = scratch[
        2 * n_chunks : 2 * n_chunks + 9
    ]
    (raw_sem, local_sem, far_send, far_recv, near_send, near_recv, sum_send, sum_recv,
     rate_send, rate_recv) = scratch[2 * n_chunks + 9 :]
    row, group = lax.axis_index("rows"), lax.axis_index("heads")
    n_rows, n_groups = lax.axis_size("rows"), lax.axis_size("heads")
    above, below = lax.rem(row + 1, n_rows), lax.rem(row + n_rows - 1, n_rows)
    peers = [lax.rem(group + step, n_groups) for step in range(1, n_groups)]
    rows_here, width = new_qkv.shape[1:]
    cache_count_here = cache_tiles.shape[1]
    tiles = rows_here // TILE
    heads = width // HEAD_DIM
    bend = n_rows // 2
    place = [(chunk, at) for chunk, count in enumerate(CHUNKS) for at in range(count)]

    def columns(head):
        return pl.ds(head * HEAD_DIM, HEAD_DIM)

    def local(source, target, sem):
        copy = pltpu.make_async_copy(source, target, sem)
        copy.start()
        return copy

    def remote(source, target, send, recv, device):
        return pltpu.make_async_remote_copy(
            src_ref=source, dst_ref=target, send_sem=send, recv_sem=recv,
            device_id=device, device_id_type=MESH,
        )

    raw_copies = [
        local(
            new_qkv.at[pl.ds(0, 2), pl.ds(t * TILE, TILE)],
            raw.at[:, pl.ds(t * TILE, TILE)],
            raw_sem.at[t],
        )
        for t in range(tiles)
    ]

    barrier = pltpu.get_barrier_semaphore()
    for device in [(above, group), (below, group)] + [(row, peer) for peer in peers]:
        pl.semaphore_signal(barrier, inc=1, device_id=device, device_id_type=MESH)
    for ones, others in (((bend - 1, bend), (0, n_rows - 1)), ((0, n_rows - 1), (bend - 1, bend))):

        @pl.when((row == ones[0]) | (row == ones[1]))
        def greet():
            for other in others:
                pl.semaphore_signal(barrier, inc=1, device_id=(other, group), device_id_type=MESH)

    ends = (row == 0) | (row == n_rows - 1) | (row == bend - 1) | (row == bend)
    pl.semaphore_wait(barrier, jnp.where(ends, n_groups + 3, n_groups + 1))

    far, near = [], []

    def exchange(head, top, bottom, low, high, send, recv):
        over_last = head % 2 == 0
        middle, at_middle = (high, (n_rows - 1, group)) if over_last else (low, (0, group))
        side = int(over_last)
        return (
            remote(top, low, send.at[head, 0], recv.at[head, 0], (above, group)),
            remote(bottom, high, send.at[head, 1], recv.at[head, 1], (below, group)),
            remote(top, middle, send.at[head, 0], recv.at[head, side], at_middle),
            remote(middle, low, send.at[head, 1 - side], recv.at[head, 0], (bend, group)),
        )

    for head, (chunk, at) in enumerate(place):
        cols = columns(head)
        there, edge = caches[chunk].at[at], news[chunk].at[at]
        far.append(
            exchange(
                head,
                cache_tiles.at[:, pl.ds(cache_count_here - REACH, REACH), :, cols],
                cache_tiles.at[:, pl.ds(0, REACH), :, cols],
                there.at[:, pl.ds(0, REACH)],
                there.at[:, pl.ds(REACH + cache_count_here, REACH)],
                far_send,
                far_recv,
            )
        )
        near.append(
            exchange(
                head,
                new_qkv.at[pl.ds(1, 2), pl.ds(rows_here - TILE, TILE), cols],
                new_qkv.at[pl.ds(1, 2), pl.ds(0, TILE), cols],
                edge.at[:, pl.ds(0, TILE)],
                edge.at[:, pl.ds(TILE + rows_here, TILE)],
                near_send,
                near_recv,
            )
        )

    def start(kind, head):
        @pl.when(row == bend - 1)
        def ahead():
            for ways in kind[2 * head : 2 * head + 2]:
                ways[2].start()

        pl.when((row < n_rows - 1) & (row != bend - 1))(kind[head][0].start)
        pl.when(row > 0)(kind[head][1].start)

    def arrive(ways):
        pl.when(row > 0)(ways[0].wait_recv)
        pl.when(row < n_rows - 1)(ways[1].wait_recv)

    def relay(pair):
        if 2 * pair >= heads:
            return

        @pl.when(row == n_rows - 1)
        def even():
            for ways in (far[2 * pair], near[2 * pair]):
                ways[1].wait_recv()
                ways[3].start()

        @pl.when(row == 0)
        def odd():
            for ways in (far[2 * pair + 1], near[2 * pair + 1]):
                ways[0].wait_recv()
                ways[3].start()

    for head in range(EARLY):
        start(far, head)

    def clear(head, line):
        chunk, at = place[head]
        news[chunk][at, :, pl.ds(line, TILE), :] = jnp.zeros((2, TILE, HEAD_DIM), jnp.bfloat16)

    @pl.when(row == 0)
    def none_below():
        for head in range(0, heads, 2):
            clear(head, 0)

    @pl.when(row == n_rows - 1)
    def none_above():
        for head in range(1, heads, 2):
            clear(head, TILE + rows_here)

    held = []
    for head, (chunk, at) in enumerate(place):
        cols = columns(head)
        held.append(
            (
                local(
                    cache_tiles.at[:, :, :, cols],
                    caches[chunk].at[at, :, pl.ds(REACH, cache_count_here)],
                    local_sem.at[head, 0],
                ),
                local(
                    new_qkv.at[2, :, cols],
                    news[chunk].at[at, 1, pl.ds(TILE, rows_here)],
                    local_sem.at[head, 1],
                ),
            )
        )

    sums[...] = jnp.zeros_like(sums)
    for t in range(tiles):
        raw_copies[t].wait()
        for which in range(2):
            total = jnp.zeros((TILE, HEAD_DIM), jnp.float32)
            for head in range(heads):
                wide = raw[which, pl.ds(t * TILE, TILE), columns(head)].astype(jnp.float32)
                total += wide * wide
            sums[pl.ds(8 * which + t, 1), :] = jnp.sum(total.T, axis=0, keepdims=True)
    sum_copies = [
        remote(sums, peer_sums.at[i], sum_send.at[i], sum_recv.at[i], (row, peer))
        for i, peer in enumerate(peers)
    ]
    for copy in sum_copies:
        copy.start()
    for copy in sum_copies:
        copy.wait_recv()
    square = sums[...]
    for i in range(len(peers)):
        square += peer_sums[i]
    rates[...] = lax.rsqrt(square / (width * n_groups) + 1e-06)
    rate_copies = [
        remote(
            rates.at[pl.ds(8, 8)], halo_rates.at[side], rate_send.at[side], rate_recv.at[side],
            (device, group),
        )
        for side, device in enumerate((above, below))
    ]
    for copy in rate_copies:
        copy.start()
    for head in range(EARLY):
        start(near, head)
    for head in range(EARLY, heads - LATE):
        start(far, head)
        start(near, head)
    for kind in (far, near):
        for head in range(heads - LATE, heads):
            start(kind, head)

    def spread(line):
        return jnp.broadcast_to(line, (TILE, TILE)).T

    for t in range(tiles):
        q_scale[t] = spread(rates[pl.ds(t, 1), :])
        k_scale[t] = spread(rates[pl.ds(8 + t, 1), :])

    dead = jnp.full((1, TILE), -jnp.inf, jnp.float32)
    lowest_new = row * tiles
    for t in range(tiles):
        live = {i: jnp.zeros((1, TILE), jnp.int32) for i in (0, 2)}
        count = jnp.full((1, TILE), new_count[t], jnp.int32)
        for j in range(1, new_list.shape[0]):
            tile = jnp.full((1, TILE), new_list[j, t], jnp.int32) - (lowest_new + t)
            for i in live:
                live[i] = jnp.where((tile == i - 1) & (count > j), 1, live[i])
        count = jnp.full((1, TILE), cache_count[t], jnp.int32)
        for j in range(1, cache_list.shape[1]):
            live[3 + j] = jnp.where(count > j, 1, 0)
        for i, line in live.items():
            bias[t, i : i + 1, :] = jnp.where(line > 0, jnp.float32(0), dead)

    lowest_cache = row * cache_count_here - REACH
    power = HEAD_DIM ** (-0.5) * 1.4426950408889634

    def attend(chunk, at, head, t, without=None):
        start = t * TILE
        cols = pl.ds(pl.multiple_of(head * HEAD_DIM, HEAD_DIM), HEAD_DIM)
        near_rows = pl.ds(start, 3 * TILE)
        if without is not None:
            near_rows = pl.ds(start + (TILE if without == 0 else 0), 2 * TILE)
        query = raw[0, pl.ds(start, TILE), cols].astype(jnp.float32)
        query = (query * q_scale[t] * q_gain[cols]).astype(jnp.bfloat16)
        far_tiles = [
            jnp.clip(cache_list[t, j] - lowest_cache, 0, cache_count_here + 2 * REACH - 1)
            for j in range(cache_list.shape[1])
        ]
        keys = [news[chunk][at, 0, near_rows, :]] + [caches[chunk][at, 0, i] for i in far_tiles]
        values = [news[chunk][at, 1, near_rows, :]] + [caches[chunk][at, 1, i] for i in far_tiles]
        scores = lax.dot_general(
            query, jnp.concatenate(keys, axis=0), (((1,), (1,)), ((), ())),
            preferred_element_type=jnp.float32,
        )
        parts = []
        for i, column in enumerate(i for i in range(3 + len(far_tiles)) if i != without):
            part = scores[:, i * TILE : (i + 1) * TILE]
            parts.append(part if column in (1, 3) else part + bias[t, column : column + 1, :])
        top = functools.reduce(jnp.maximum, parts)
        top = jnp.max(top, axis=1, keepdims=True)
        weights = [jnp.exp2((part - top) * power) for part in parts]
        total = jnp.sum(functools.reduce(jnp.add, weights), axis=1, keepdims=True)
        weights = jnp.concatenate([w.astype(jnp.bfloat16) for w in weights], axis=1)
        result = jnp.dot(
            weights, jnp.concatenate(values, axis=0), preferred_element_type=jnp.float32
        )
        if without is not None:
            return query, top, total, result
        out[pl.ds(start, TILE), cols] = (result / total).astype(jnp.bfloat16)

    def finish(chunk, at, head, t, without, query, top, total, result):
        cols = pl.ds(head * HEAD_DIM, HEAD_DIM)
        halo = pl.ds((t + without) * TILE, TILE)
        scores = lax.dot_general(
            query, news[chunk][at, 0, halo, :], (((1,), (1,)), ((), ())),
            preferred_element_type=jnp.float32,
        )
        scores += bias[t, without : without + 1, :]
        peak = jnp.maximum(top, jnp.max(scores, axis=1, keepdims=True))
        weights = jnp.exp2((scores - peak) * power)
        fade = jnp.exp2((top - peak) * power)
        total = total * fade + jnp.sum(weights, axis=1, keepdims=True)
        result = result * fade + jnp.dot(
            weights.astype(jnp.bfloat16), news[chunk][at, 1, halo, :],
            preferred_element_type=jnp.float32,
        )
        out[pl.ds(t * TILE, TILE), cols] = (result / total).astype(jnp.bfloat16)

    def normed_keys(head, t):
        cols = pl.ds(pl.multiple_of(head * HEAD_DIM, HEAD_DIM), HEAD_DIM)
        wide = raw[1, pl.ds(t * TILE, TILE), cols].astype(jnp.float32)
        return (wide * k_scale[t] * k_gain[cols]).astype(jnp.bfloat16)

    firsts = [sum(CHUNKS[:chunk]) for chunk in range(n_chunks)]

    def inner(chunk):
        first, count = firsts[chunk], CHUNKS[chunk]
        for head in range(first, first + count):
            for copy in held[head]:
                copy.wait()
            arrive(far[head])
        relay(2 * chunk)

        @pl.loop(0, count)
        def one(at):
            head = first + at
            for t in range(tiles):
                news[chunk][at, 0, pl.ds((t + 1) * TILE, TILE), :] = normed_keys(head, t)
            for t in range(1, tiles - 1):
                attend(chunk, at, head, t)

    def outer(chunk):
        first, count = firsts[chunk], CHUNKS[chunk]
        if chunk == 0:
            for copy in rate_copies:
                copy.wait_recv()
            halo_scale[0] = spread(halo_rates[0, pl.ds(tiles - 1, 1), :])
            halo_scale[1] = spread(halo_rates[1, pl.ds(0, 1), :])
        for head in range(first, first + count):
            arrive(near[head])
        relay(2 * chunk + 1)

        @pl.loop(0, count)
        def one(at):
            head = first + at
            norm_halos(chunk, at, head)
            for t in (0, tiles - 1):
                attend(chunk, at, head, t)

    def norm_halos(chunk, at, head):
        cols = pl.ds(pl.multiple_of(head * HEAD_DIM, HEAD_DIM), HEAD_DIM)

        def norm_halo(side):
            where = pl.ds(side * (TILE + rows_here), TILE)
            wide = news[chunk][at, 0, where, :].astype(jnp.float32)
            news[chunk][at, 0, where, :] = (wide * halo_scale[side] * k_gain[cols]).astype(
                jnp.bfloat16
            )

        pl.when(row > 0)(lambda: norm_halo(0))
        pl.when(row < n_rows - 1)(lambda: norm_halo(1))

    for chunk in range(n_chunks - LATE):
        inner(chunk)
        outer(chunk)
    for chunk in range(n_chunks - LATE, n_chunks):
        inner(chunk)
    chunk, head = n_chunks - 1, heads - 1
    sides = ((0, 0), (tiles - 1, 2))
    begun = [attend(chunk, 0, head, t, without) for t, without in sides]
    for before in range(n_chunks - LATE, n_chunks - 1):
        outer(before)
    arrive(near[head])
    norm_halos(chunk, 0, head)
    for (t, without), state in zip(sides, begun):
        finish(chunk, 0, head, t, without, *state)

    for copy in sum_copies + rate_copies:
        copy.wait_send()
    for head in range(heads):
        for ways in (far[head], near[head]):
            if head % 2 == 0:
                ways[0].wait_send()
                pl.when(row > 0)(ways[1].wait_send)
            else:
                pl.when(row < n_rows - 1)(ways[0].wait_send)
                ways[1].wait_send()


def on_device(new_qkv, cache_kv, q_gain, k_gain, new_list, new_count, cache_list, cache_count):
    rows_here, width = new_qkv.shape[1:]
    cache_rows = cache_kv.shape[1]
    tiles = rows_here // TILE
    heads = width // HEAD_DIM
    groups = lax.axis_size("heads")
    in_smem = pl.BlockSpec(memory_space=pltpu.SMEM)
    in_vmem = pl.BlockSpec(memory_space=pltpu.VMEM)
    anywhere = pl.BlockSpec(memory_space=pl.ANY)
    dma = pltpu.SemaphoreType.DMA
    keys_here = (tiles + 3 + cache_list.shape[1]) * TILE
    return pl.pallas_call(
        kernel,
        out_shape=pltpu.VMEM((rows_here, width), jnp.bfloat16),
        in_specs=[in_smem] * 4 + [in_vmem] * 2 + [anywhere] * 2,
        out_specs=in_vmem,
        scratch_shapes=[
            pltpu.VMEM((count, 2, rows_here + 2 * TILE, HEAD_DIM), jnp.bfloat16)
            for count in CHUNKS
        ]
        + [
            pltpu.VMEM((count, 2, cache_rows // TILE + 2 * REACH, TILE, HEAD_DIM), jnp.bfloat16)
            for count in CHUNKS
        ]
        + [
            pltpu.VMEM((2, rows_here, width), jnp.bfloat16),
            pltpu.VMEM((tiles, TILE, HEAD_DIM), jnp.float32),
            pltpu.VMEM((tiles, TILE, HEAD_DIM), jnp.float32),
            pltpu.VMEM((2, TILE, HEAD_DIM), jnp.float32),
            pltpu.VMEM((16, TILE), jnp.float32),
            pltpu.VMEM((groups - 1, 16, TILE), jnp.float32),
            pltpu.VMEM((16, TILE), jnp.float32),
            pltpu.VMEM((2, 8, TILE), jnp.float32),
            pltpu.VMEM((tiles, 3 + cache_list.shape[1], TILE), jnp.float32),
            dma((tiles,)),
            dma((heads, 2)),
            dma((heads, 2)),
            dma((heads, 2)),
            dma((heads, 2)),
            dma((heads, 2)),
            dma((groups - 1,)),
            dma((groups - 1,)),
            dma((2,)),
            dma((2,)),
        ],
        compiler_params=pltpu.CompilerParams(
            collective_id=0, has_side_effects=True, vmem_limit_bytes=60 * 2**20
        ),
        cost_estimate=pl.CostEstimate(
            flops=4 * rows_here * keys_here * width,
            bytes_accessed=2 * (4 * rows_here + 2 * cache_rows) * width,
            transcendentals=rows_here * keys_here * heads,
        ),
    )(
        new_list.T,
        new_count,
        cache_list,
        cache_count,
        q_gain,
        k_gain,
        new_qkv,
        cache_kv.reshape(2, cache_rows // TILE, TILE, width),
    )


def solution(mesh):
    placed = (
        P(None, "rows", "heads"),
        P(None, "rows", "heads"),
        P("heads"),
        P("heads"),
        P("rows", None),
        P("rows"),
        P("rows", None),
        P("rows"),
    )
    return jax.shard_map(
        on_device, mesh=mesh, in_specs=placed, out_specs=P("rows", "heads"), check_vma=False
    )
```

```python
import functools

import jax
import jax.numpy as jnp
from jax import lax
from jax.experimental import pallas as pl
from jax.experimental.pallas import tpu as pltpu
from jax.sharding import PartitionSpec as P

HEADS = 40
HEAD_DIM = 128
TILE = 128
REACH = 2
CHUNKS = (2, 2, 2, 1, 1, 1, 1)
LATE = 3
EARLY = 3
MESH = pl.DeviceIdType.MESH


def kernel(
    new_list, new_count, cache_list, cache_count, q_gain, k_gain, new_qkv, cache_tiles, out, *scratch
):
    n_chunks = len(CHUNKS)
    news, caches = scratch[:n_chunks], scratch[n_chunks : 2 * n_chunks]
    (raw, q_scale, k_scale, halo_scale, sums, peer_sums, rates, halo_rates, bias) = scratch[
        2 * n_chunks : 2 * n_chunks + 9
    ]
    (raw_sem, local_sem, far_send, far_recv, near_send, near_recv, sum_send, sum_recv,
     rate_send, rate_recv) = scratch[2 * n_chunks + 9 :]
    row, group = lax.axis_index("rows"), lax.axis_index("heads")
    n_rows, n_groups = lax.axis_size("rows"), lax.axis_size("heads")
    above, below = lax.rem(row + 1, n_rows), lax.rem(row + n_rows - 1, n_rows)
    peers = [lax.rem(group + step, n_groups) for step in range(1, n_groups)]
    rows_here, width = new_qkv.shape[1:]
    cache_count_here = cache_tiles.shape[1]
    tiles = rows_here // TILE
    heads = width // HEAD_DIM
    bend = n_rows // 2
    place = [(chunk, at) for chunk, count in enumerate(CHUNKS) for at in range(count)]

    def columns(head):
        return pl.ds(head * HEAD_DIM, HEAD_DIM)

    def local(source, target, sem):
        copy = pltpu.make_async_copy(source, target, sem)
        copy.start()
        return copy

    def remote(source, target, send, recv, device):
        return pltpu.make_async_remote_copy(
            src_ref=source, dst_ref=target, send_sem=send, recv_sem=recv,
            device_id=device, device_id_type=MESH,
        )

    raw_copies = [
        local(
            new_qkv.at[pl.ds(0, 2), pl.ds(t * TILE, TILE)],
            raw.at[:, pl.ds(t * TILE, TILE)],
            raw_sem.at[t],
        )
        for t in range(tiles)
    ]

    barrier = pltpu.get_barrier_semaphore()
    def greet(device):
        pl.semaphore_signal(barrier, inc=1, device_id=device, device_id_type=MESH)

    pl.when(row < n_rows - 1)(lambda: greet((above, group)))
    pl.when(row > 0)(lambda: greet((below, group)))
    for peer in peers:
        greet((row, peer))
    pl.when((row == 0) | (row == n_rows - 1))(lambda: greet((bend - 1, group)))

    @pl.when(row == bend)
    def greet_ends():
        greet((0, group))
        greet((n_rows - 1, group))

    pl.semaphore_wait(barrier, jnp.where(row == bend - 1, n_groups + 3, n_groups + 1))

    far, near = [], []

    def exchange(head, top, bottom, low, high, send, recv):
        over_last = head % 2 == 0
        middle, at_middle = (high, (n_rows - 1, group)) if over_last else (low, (0, group))
        side = int(over_last)
        return (
            remote(top, low, send.at[head, 0], recv.at[head, 0], (above, group)),
            remote(bottom, high, send.at[head, 1], recv.at[head, 1], (below, group)),
            remote(top, middle, send.at[head, 0], recv.at[head, side], at_middle),
            remote(middle, low, send.at[head, 1 - side], recv.at[head, 0], (bend, group)),
        )

    for head, (chunk, at) in enumerate(place):
        cols = columns(head)
        there, edge = caches[chunk].at[at], news[chunk].at[at]
        far.append(
            exchange(
                head,
                cache_tiles.at[:, pl.ds(cache_count_here - REACH, REACH), :, cols],
                cache_tiles.at[:, pl.ds(0, REACH), :, cols],
                there.at[:, pl.ds(0, REACH)],
                there.at[:, pl.ds(REACH + cache_count_here, REACH)],
                far_send,
                far_recv,
            )
        )
        near.append(
            exchange(
                head,
                new_qkv.at[pl.ds(1, 2), pl.ds(rows_here - TILE, TILE), cols],
                new_qkv.at[pl.ds(1, 2), pl.ds(0, TILE), cols],
                edge.at[:, pl.ds(0, TILE)],
                edge.at[:, pl.ds(TILE + rows_here, TILE)],
                near_send,
                near_recv,
            )
        )

    def start(kind, head):
        @pl.when(row == bend - 1)
        def ahead():
            for ways in kind[2 * head : 2 * head + 2]:
                ways[2].start()

        pl.when((row < n_rows - 1) & (row != bend - 1))(kind[head][0].start)
        pl.when(row > 0)(kind[head][1].start)

    def arrive(ways):
        pl.when(row > 0)(ways[0].wait_recv)
        pl.when(row < n_rows - 1)(ways[1].wait_recv)

    def relay(pair):
        if 2 * pair >= heads:
            return

        @pl.when(row == n_rows - 1)
        def even():
            for ways in (far[2 * pair], near[2 * pair]):
                ways[1].wait_recv()
                ways[3].start()

        @pl.when(row == 0)
        def odd():
            for ways in (far[2 * pair + 1], near[2 * pair + 1]):
                ways[0].wait_recv()
                ways[3].start()

    for head in range(EARLY):
        start(far, head)

    def clear(head, line):
        chunk, at = place[head]
        news[chunk][at, :, pl.ds(line, TILE), :] = jnp.zeros((2, TILE, HEAD_DIM), jnp.bfloat16)

    @pl.when(row == 0)
    def none_below():
        for head in range(0, heads, 2):
            clear(head, 0)

    @pl.when(row == n_rows - 1)
    def none_above():
        for head in range(1, heads, 2):
            clear(head, TILE + rows_here)

    held = []
    for head, (chunk, at) in enumerate(place):
        cols = columns(head)
        held.append(
            (
                local(
                    cache_tiles.at[:, :, :, cols],
                    caches[chunk].at[at, :, pl.ds(REACH, cache_count_here)],
                    local_sem.at[head, 0],
                ),
                local(
                    new_qkv.at[2, :, cols],
                    news[chunk].at[at, 1, pl.ds(TILE, rows_here)],
                    local_sem.at[head, 1],
                ),
            )
        )

    sums[...] = jnp.zeros_like(sums)
    for t in range(tiles):
        raw_copies[t].wait()
        for which in range(2):
            total = jnp.zeros((TILE, HEAD_DIM), jnp.float32)
            for head in range(heads):
                wide = raw[which, pl.ds(t * TILE, TILE), columns(head)].astype(jnp.float32)
                total += wide * wide
            sums[pl.ds(8 * which + t, 1), :] = jnp.sum(total.T, axis=0, keepdims=True)
    sum_copies = [
        remote(sums, peer_sums.at[i], sum_send.at[i], sum_recv.at[i], (row, peer))
        for i, peer in enumerate(peers)
    ]
    for copy in sum_copies:
        copy.start()
    for copy in sum_copies:
        copy.wait_recv()
    square = sums[...]
    for i in range(len(peers)):
        square += peer_sums[i]
    rates[...] = lax.rsqrt(square / (width * n_groups) + 1e-06)
    rate_copies = [
        remote(
            rates.at[pl.ds(8, 8)], halo_rates.at[side], rate_send.at[side], rate_recv.at[side],
            (device, group),
        )
        for side, device in enumerate((above, below))
    ]
    pl.when(row < n_rows - 1)(rate_copies[0].start)
    pl.when(row > 0)(rate_copies[1].start)
    for head in range(EARLY):
        start(near, head)
    for head in range(EARLY, heads - LATE):
        start(far, head)
        start(near, head)
    for kind in (far, near):
        for head in range(heads - LATE, heads):
            start(kind, head)

    def spread(line):
        return jnp.broadcast_to(line, (TILE, TILE)).T

    for t in range(tiles):
        q_scale[t] = spread(rates[pl.ds(t, 1), :])
        k_scale[t] = spread(rates[pl.ds(8 + t, 1), :])

    dead = jnp.full((1, TILE), -jnp.inf, jnp.float32)
    lowest_new = row * tiles
    for t in range(tiles):
        live = {i: jnp.zeros((1, TILE), jnp.int32) for i in (0, 2)}
        count = jnp.full((1, TILE), new_count[t], jnp.int32)
        for j in range(1, new_list.shape[0]):
            tile = jnp.full((1, TILE), new_list[j, t], jnp.int32) - (lowest_new + t)
            for i in live:
                live[i] = jnp.where((tile == i - 1) & (count > j), 1, live[i])
        count = jnp.full((1, TILE), cache_count[t], jnp.int32)
        for j in range(1, cache_list.shape[1]):
            live[3 + j] = jnp.where(count > j, 1, 0)
        for i, line in live.items():
            bias[t, i : i + 1, :] = jnp.where(line > 0, jnp.float32(0), dead)

    lowest_cache = row * cache_count_here - REACH
    power = HEAD_DIM ** (-0.5) * 1.4426950408889634

    def attend(chunk, at, head, t, without=None):
        start = t * TILE
        cols = pl.ds(pl.multiple_of(head * HEAD_DIM, HEAD_DIM), HEAD_DIM)
        near_rows = pl.ds(start, 3 * TILE)
        if without is not None:
            near_rows = pl.ds(start + (TILE if without == 0 else 0), 2 * TILE)
        query = raw[0, pl.ds(start, TILE), cols].astype(jnp.float32)
        query = (query * q_scale[t] * q_gain[cols]).astype(jnp.bfloat16)
        far_tiles = [
            jnp.clip(cache_list[t, j] - lowest_cache, 0, cache_count_here + 2 * REACH - 1)
            for j in range(cache_list.shape[1])
        ]
        keys = [news[chunk][at, 0, near_rows, :]] + [caches[chunk][at, 0, i] for i in far_tiles]
        values = [news[chunk][at, 1, near_rows, :]] + [caches[chunk][at, 1, i] for i in far_tiles]
        scores = lax.dot_general(
            query, jnp.concatenate(keys, axis=0), (((1,), (1,)), ((), ())),
            preferred_element_type=jnp.float32,
        )
        parts = []
        for i, column in enumerate(i for i in range(3 + len(far_tiles)) if i != without):
            part = scores[:, i * TILE : (i + 1) * TILE]
            parts.append(part if column in (1, 3) else part + bias[t, column : column + 1, :])
        top = functools.reduce(jnp.maximum, parts)
        top = jnp.max(top, axis=1, keepdims=True)
        weights = [jnp.exp2((part - top) * power) for part in parts]
        total = jnp.sum(functools.reduce(jnp.add, weights), axis=1, keepdims=True)
        weights = jnp.concatenate([w.astype(jnp.bfloat16) for w in weights], axis=1)
        result = jnp.dot(
            weights, jnp.concatenate(values, axis=0), preferred_element_type=jnp.float32
        )
        if without is not None:
            return query, top, total, result
        out[pl.ds(start, TILE), cols] = (result / total).astype(jnp.bfloat16)

    def finish(chunk, at, head, t, without, query, top, total, result):
        cols = pl.ds(head * HEAD_DIM, HEAD_DIM)
        halo = pl.ds((t + without) * TILE, TILE)
        scores = lax.dot_general(
            query, news[chunk][at, 0, halo, :], (((1,), (1,)), ((), ())),
            preferred_element_type=jnp.float32,
        )
        scores += bias[t, without : without + 1, :]
        peak = jnp.maximum(top, jnp.max(scores, axis=1, keepdims=True))
        weights = jnp.exp2((scores - peak) * power)
        fade = jnp.exp2((top - peak) * power)
        total = total * fade + jnp.sum(weights, axis=1, keepdims=True)
        result = result * fade + jnp.dot(
            weights.astype(jnp.bfloat16), news[chunk][at, 1, halo, :],
            preferred_element_type=jnp.float32,
        )
        out[pl.ds(t * TILE, TILE), cols] = (result / total).astype(jnp.bfloat16)

    def normed_keys(head, t):
        cols = pl.ds(pl.multiple_of(head * HEAD_DIM, HEAD_DIM), HEAD_DIM)
        wide = raw[1, pl.ds(t * TILE, TILE), cols].astype(jnp.float32)
        return (wide * k_scale[t] * k_gain[cols]).astype(jnp.bfloat16)

    firsts = [sum(CHUNKS[:chunk]) for chunk in range(n_chunks)]

    def inner(chunk):
        first, count = firsts[chunk], CHUNKS[chunk]
        for head in range(first, first + count):
            for copy in held[head]:
                copy.wait()
            arrive(far[head])
        relay(2 * chunk)

        @pl.loop(0, count)
        def one(at):
            head = first + at
            for t in range(tiles):
                news[chunk][at, 0, pl.ds((t + 1) * TILE, TILE), :] = normed_keys(head, t)
            for t in range(1, tiles - 1):
                attend(chunk, at, head, t)

    def outer(chunk):
        first, count = firsts[chunk], CHUNKS[chunk]
        if chunk == 0:
            pl.when(row > 0)(rate_copies[0].wait_recv)
            pl.when(row < n_rows - 1)(rate_copies[1].wait_recv)
            halo_scale[0] = spread(halo_rates[0, pl.ds(tiles - 1, 1), :])
            halo_scale[1] = spread(halo_rates[1, pl.ds(0, 1), :])
        for head in range(first, first + count):
            arrive(near[head])
        relay(2 * chunk + 1)

        @pl.loop(0, count)
        def one(at):
            head = first + at
            norm_halos(chunk, at, head)
            for t in (0, tiles - 1):
                attend(chunk, at, head, t)

    def norm_halos(chunk, at, head):
        cols = pl.ds(pl.multiple_of(head * HEAD_DIM, HEAD_DIM), HEAD_DIM)

        def norm_halo(side):
            where = pl.ds(side * (TILE + rows_here), TILE)
            wide = news[chunk][at, 0, where, :].astype(jnp.float32)
            news[chunk][at, 0, where, :] = (wide * halo_scale[side] * k_gain[cols]).astype(
                jnp.bfloat16
            )

        pl.when(row > 0)(lambda: norm_halo(0))
        pl.when(row < n_rows - 1)(lambda: norm_halo(1))

    for chunk in range(n_chunks - LATE):
        inner(chunk)
        outer(chunk)
    for chunk in range(n_chunks - LATE, n_chunks):
        inner(chunk)
    chunk, head = n_chunks - 1, heads - 1
    sides = ((0, 0), (tiles - 1, 2))
    begun = [attend(chunk, 0, head, t, without) for t, without in sides]
    for before in range(n_chunks - LATE, n_chunks - 1):
        outer(before)
    arrive(near[head])
    norm_halos(chunk, 0, head)
    for (t, without), state in zip(sides, begun):
        finish(chunk, 0, head, t, without, *state)

    for copy in sum_copies:
        copy.wait_send()
    pl.when(row < n_rows - 1)(rate_copies[0].wait_send)
    pl.when(row > 0)(rate_copies[1].wait_send)
    for head in range(heads):
        for ways in (far[head], near[head]):
            if head % 2 == 0:
                ways[0].wait_send()
                pl.when(row > 0)(ways[1].wait_send)
            else:
                pl.when(row < n_rows - 1)(ways[0].wait_send)
                ways[1].wait_send()


def on_device(new_qkv, cache_kv, q_gain, k_gain, new_list, new_count, cache_list, cache_count):
    rows_here, width = new_qkv.shape[1:]
    cache_rows = cache_kv.shape[1]
    tiles = rows_here // TILE
    heads = width // HEAD_DIM
    groups = lax.axis_size("heads")
    in_smem = pl.BlockSpec(memory_space=pltpu.SMEM)
    in_vmem = pl.BlockSpec(memory_space=pltpu.VMEM)
    anywhere = pl.BlockSpec(memory_space=pl.ANY)
    dma = pltpu.SemaphoreType.DMA
    keys_here = (tiles + 3 + cache_list.shape[1]) * TILE
    return pl.pallas_call(
        kernel,
        out_shape=pltpu.VMEM((rows_here, width), jnp.bfloat16),
        in_specs=[in_smem] * 4 + [in_vmem] * 2 + [anywhere] * 2,
        out_specs=in_vmem,
        scratch_shapes=[
            pltpu.VMEM((count, 2, rows_here + 2 * TILE, HEAD_DIM), jnp.bfloat16)
            for count in CHUNKS
        ]
        + [
            pltpu.VMEM((count, 2, cache_rows // TILE + 2 * REACH, TILE, HEAD_DIM), jnp.bfloat16)
            for count in CHUNKS
        ]
        + [
            pltpu.VMEM((2, rows_here, width), jnp.bfloat16),
            pltpu.VMEM((tiles, TILE, HEAD_DIM), jnp.float32),
            pltpu.VMEM((tiles, TILE, HEAD_DIM), jnp.float32),
            pltpu.VMEM((2, TILE, HEAD_DIM), jnp.float32),
            pltpu.VMEM((16, TILE), jnp.float32),
            pltpu.VMEM((groups - 1, 16, TILE), jnp.float32),
            pltpu.VMEM((16, TILE), jnp.float32),
            pltpu.VMEM((2, 8, TILE), jnp.float32),
            pltpu.VMEM((tiles, 3 + cache_list.shape[1], TILE), jnp.float32),
            dma((tiles,)),
            dma((heads, 2)),
            dma((heads, 2)),
            dma((heads, 2)),
            dma((heads, 2)),
            dma((heads, 2)),
            dma((groups - 1,)),
            dma((groups - 1,)),
            dma((2,)),
            dma((2,)),
        ],
        compiler_params=pltpu.CompilerParams(
            collective_id=0, has_side_effects=True, vmem_limit_bytes=60 * 2**20
        ),
        cost_estimate=pl.CostEstimate(
            flops=4 * rows_here * keys_here * width,
            bytes_accessed=2 * (4 * rows_here + 2 * cache_rows) * width,
            transcendentals=rows_here * keys_here * heads,
        ),
    )(
        new_list.T,
        new_count,
        cache_list,
        cache_count,
        q_gain,
        k_gain,
        new_qkv,
        cache_kv.reshape(2, cache_rows // TILE, TILE, width),
    )


def solution(mesh):
    placed = (
        P(None, "rows", "heads"),
        P(None, "rows", "heads"),
        P("heads"),
        P("heads"),
        P("rows", None),
        P("rows"),
        P("rows", None),
        P("rows"),
    )
    return jax.shard_map(
        on_device, mesh=mesh, in_specs=placed, out_specs=P("rows", "heads"), check_vma=False
    )
```
